32 devices in a mesh: groups: 2 (over x), pts: 8 (over z, y), sub: 2 (over core).
Axes of the slice: x: 2, y: 2, z: 4, core: 2. Of those that a mesh axis runs over, the one named last changes fastest.
Arguments:
- points: float32 [8192, 64], P(('groups', 'pts', 'sub')), parts along dimension 0, may hold values from -6 to 6
- inverse_scale: float32 [64], replicated, may hold values from 0.03 to 0.15
- noise_level: float32 [8192], P(('groups', 'pts', 'sub')), parts along dimension 0, may hold values from 0.3 to 3
- probes: float32 [8192, 32], P(('groups', 'pts', 'sub')), parts along dimension 0, may hold values from -6 to 6
- task_cov: float32 [8, 8], replicated, may hold values from 0 to 1.5, as said below
Outputs:
- solution: float32 [8192, 32], P(('groups', 'pts', 'sub')), parts along dimension 0
- residual: float32 [8192, 32], P(('groups', 'pts', 'sub')), parts along dimension 0
The draws below stay inside these ranges and needn't reach their ends.
There are 2 independent parts, one for each index of `groups`. The reference program is written for one: setup_inputs(seed, part) draws one part's arguments, and reference() takes and returns one part's arrays. A program takes and returns all parts, laid end to end along the dimension named above; an argument that names none is the same for every part. Nothing has to cross between parts.
Inputs may be any that keep to these rules, and one draw needn't show every extreme that they name: task_cov is symmetric with positive entries, and each diagonal entry exceeds the sum of the other entries of its row.
All inputs are finite; a program needn't handle non-finite values.
Results may differ from the reference program's by a relative error of at most 0.0003.
Values sent between devices are 32-bit elements; how exact they have to be, the bound alone decides.
A program may use at most 64 MiB of HBM per device.

```python
import math
import jax
import jax.numpy as jnp
from jax import lax

FEATURES = 64
VECTORS = 32
ITERS = 3
POINTS = 4096
N_PTS = 8


def draw_task_cov(key, part):
    key = jax.random.fold_in(key, 11)
    key_off, key_diag = jax.random.split(key)
    blocks = N_PTS
    raw = jax.random.uniform(key_off, (blocks, blocks), jnp.float32, 0.5, 1.0)
    diag = jax.random.uniform(key_diag, (blocks,), jnp.float32, 1.0, 1.5)
    off = 0.45 * (raw + raw.T) / (blocks - 1)
    eye = jnp.eye(blocks, dtype=jnp.float32)
    return off * (1.0 - eye) + eye * diag[None, :]


def shard_levels(rng, dims, cuts, least, largest):
    level = 1.0
    for dim, shards_of in cuts:
        draws = jax.random.uniform(jax.random.fold_in(jax.random.fold_in(rng, 6), dim), (shards_of,), jnp.float32, least / len(cuts), largest / len(cuts))
        level = level * jnp.repeat(jnp.exp(draws), dims[dim] // shards_of).reshape((-1,) + (1,) * (len(dims) - 1 - dim))
    return level


def centred(rng, extent, scale, limit, cuts=(), kind=jnp.bfloat16):
    loudness = shard_levels(rng, extent, cuts, -0.22, 0.18) if cuts else 1.0
    entries = jax.random.normal(rng, extent, jnp.float32) * scale * loudness
    return jnp.minimum(jnp.maximum(entries, -limit), limit).astype(kind)


def setup_inputs(seed: int = 0, part: int = 0) -> dict:
    seeds = jax.random.split(jax.random.key(seed), 6)
    part_keys = jax.random.split(jax.random.fold_in(seeds[5], part), 6)
    points = centred(part_keys[0], (POINTS, FEATURES), 1.0, 6.0, ((0, 16),), jnp.float32)
    inverse_scale = jnp.clip(jnp.exp(jax.random.uniform(seeds[1], (FEATURES,), jnp.float32, math.log(0.03), math.log(0.15))), 0.03, 0.15)
    noise_level = jnp.clip(jnp.exp(math.log(3.0) - 2.3025851 * jax.random.uniform(part_keys[2], (POINTS,), jnp.float32) ** shard_levels(part_keys[2], (POINTS,), ((0, 16),), -0.2, 0.2)), 0.3, 3.0)
    probes = centred(part_keys[3], (POINTS, VECTORS), 1.0, 6.0, ((0, 16),), jnp.float32)
    task_cov = draw_task_cov(jax.random.fold_in(seeds[5], 71), part)
    return dict(points=points, inverse_scale=inverse_scale, noise_level=noise_level, probes=probes, task_cov=task_cov)


SQRT_FIVE = 5.0 ** 0.5
HIGHEST = lax.Precision.HIGHEST

def matern(rows_scaled, rows_square, cols_scaled, cols_square):
    inner = lax.dot_general(rows_scaled, cols_scaled, (((1,), (1,)), ((), ())), precision=HIGHEST, preferred_element_type=jnp.float32)
    squared = jnp.maximum(rows_square[:, None] + cols_square[None, :] - 2.0 * inner, 0.0)
    distance = jnp.sqrt(squared)
    return (1.0 + SQRT_FIVE * distance + 5.0 / 3.0 * squared) * jnp.exp(-SQRT_FIVE * distance)

def apply_kernel(scaled, square, noise_level, weights, vector):
    blocks = weights.shape[0]
    total = scaled.shape[0]
    width = total // blocks
    column_weights = jnp.repeat(weights, width, axis=1)

    def one_block(inputs):
        block_scaled, block_square, block_weights = inputs
        tile = matern(block_scaled, block_square, scaled, square) * block_weights[None, :]
        return jnp.dot(tile, vector, precision=HIGHEST, preferred_element_type=jnp.float32)
    image = lax.map(one_block, (scaled.reshape(blocks, width, scaled.shape[1]), square.reshape(blocks, width), column_weights))
    return image.reshape(total, vector.shape[1]) + noise_level[:, None] * vector

def reference(points, inverse_scale, noise_level, probes, task_cov):
    scaled = points * inverse_scale[None, :]
    square = lax.optimization_barrier(jnp.sum(scaled * scaled, axis=1))
    solution = jnp.zeros_like(probes)
    residual = probes
    direction = probes
    norm_now = lax.optimization_barrier(jnp.sum(residual * residual, axis=0))
    for iteration in range(ITERS):
        image = apply_kernel(scaled, square, noise_level, task_cov, direction)
        alpha = norm_now / lax.optimization_barrier(jnp.sum(direction * image, axis=0))
        solution = solution + alpha[None, :] * direction
        residual = residual - alpha[None, :] * image
        norm_next = lax.optimization_barrier(jnp.sum(residual * residual, axis=0))
        direction = residual + (norm_next / norm_now)[None, :] * direction
        norm_now = norm_next
    return (solution, residual)
```

```python
import functools

import jax
import jax.numpy as jnp
from jax import lax
from jax.experimental import pallas as pl
from jax.experimental.pallas import tpu as pltpu
from jax.sharding import PartitionSpec as P

ITERS = 3
PAIR = 2
MESH = pl.DeviceIdType.MESH
SQRT_FIVE = 5.0**0.5
F32, BF16 = jnp.float32, jnp.bfloat16


def halves(x):
    hi = x.astype(BF16)
    return hi, (x - hi.astype(F32)).astype(BF16)


def augmented(scaled):
    features, width = scaled.shape
    hi, lo = (part.astype(F32) for part in halves(scaled))
    square = jnp.sum(hi * hi + 2.0 * (hi * lo), axis=0, keepdims=True)
    top, rest = (part.astype(F32) for part in halves(square))
    mid = rest
    low = square - top - mid
    pad = (-3 * features) % 128
    row = lax.broadcasted_iota(jnp.int32, (pad, width), 0)
    three = jnp.where(row % 3 == 0, top, jnp.where(row % 3 == 1, mid, low))
    one = jnp.ones_like(three)
    zero = jnp.zeros_like(three)
    left = jnp.where(row < 3, three, jnp.where(row < 6, one, zero))
    right = jnp.where(row < 3, one, jnp.where(row < 6, three, zero))
    return (
        jnp.concatenate([-2.0 * hi, -2.0 * hi, -2.0 * lo, left], axis=0),
        jnp.concatenate([hi, lo, hi, right], axis=0),
    )


def kernel(
    nz, ny, ns, points_ref, inverse_ref, noise_ref, probes_ref, weights_ref, sol_ref, res_ref,
    col_pts, row_pts, vec, part_out, part, rr_buf, dot_buf, k_hi, k_lo, right_fac, sq_dist,
    pts_z_send, pts_z_recv, pts_q_send, pts_q_recv, vec_send, vec_recv,
    part_send, part_recv, rr_send, rr_recv, dot_send, dot_recv,
):
    n, m = probes_ref.shape
    nq = ny * ns
    block = lax.axis_index("pts")
    core = lax.axis_index("sub")
    z, y = block // ny, block % ny

    def device(dz, a, b):
        return {"pts": ((z + dz) % nz) * ny + (y + a) % ny, "sub": (core + b) % ns}

    q_offsets = [(a, b) for a in range(ny) for b in range(ns)]
    offsets = [(dz, a, b) for dz in range(nz) for a, b in q_offsets]

    def mirror_q(j):
        a, b = q_offsets[j]
        return ((-a) % ny) * ns + (-b) % ns

    def mirror(i):
        dz, a, b = offsets[i]
        return ((-dz) % nz) * nq + mirror_q(a * ns + b)

    sends = []

    def send(src, dst, send_sem, recv_sem, target):
        copy = pltpu.make_async_remote_copy(
            src_ref=src, dst_ref=dst, send_sem=send_sem, recv_sem=recv_sem,
            device_id=target, device_id_type=MESH,
        )
        copy.start()
        sends.append(copy)

    def arrived(dst, send_sem, recv_sem):
        pltpu.make_async_remote_copy(
            src_ref=dst, dst_ref=dst, send_sem=send_sem, recv_sem=recv_sem,
            device_id=device(1, 0, 0), device_id_type=MESH,
        ).wait_recv()

    barrier = pltpu.get_barrier_semaphore()
    for i in range(1, nz * nq):
        pl.semaphore_signal(barrier, inc=1, device_id=device(*offsets[i]), device_id_type=MESH)

    scaled = (points_ref[...] * (inverse_ref[...] * SQRT_FIVE)).T
    col_pts[0] = scaled
    own_probes = probes_ref[...].T
    vec[0, 0] = own_probes

    pl.semaphore_wait(barrier, nz * nq - 1)

    for dz in range(1, nz):
        k = nz - dz
        send(col_pts.at[0], col_pts.at[k], pts_z_send.at[k], pts_z_recv.at[k], device(dz, 0, 0))
    for j in range(1, nq):
        k = mirror_q(j)
        send(col_pts.at[0], row_pts.at[k], pts_q_send.at[k], pts_q_recv.at[k], device(0, *q_offsets[j]))

    def gather_vector(t):
        for dz in range(1, nz):
            k = nz - dz
            send(vec.at[t, 0], vec.at[t, k], vec_send.at[t, k], vec_recv.at[t, k], device(dz, 0, 0))

    def vector_block(t, k):
        if k:
            arrived(vec.at[t, k], vec_send.at[t, k], vec_recv.at[t, k])
        return vec[t, k]

    gather_vector(0)

    for j in range(nq):
        if j:
            arrived(row_pts.at[j], pts_q_send.at[j], pts_q_recv.at[j])
            factor = augmented(row_pts[j])[1]
        else:
            factor = augmented(scaled)[1]
        right_fac[:, j * n:(j + 1) * n] = factor.astype(BF16)

    half = ns * n
    for k in range(nz):
        if k:
            arrived(col_pts.at[k], pts_z_send.at[k], pts_z_recv.at[k])
        left = augmented(col_pts[k])[0].T.astype(BF16)
        sq_dist[...] = jnp.dot(left, right_fac[...], preferred_element_type=F32)
        column_block = ((z + k) % nz) * ny + y
        weight = [weights_ref[z * ny + (y + a) % ny, column_block] for a in range(ny)]

        def rows(i, carry):
            at = pl.multiple_of(i * 16, 16)
            for a in range(ny):
                span = slice(a * half, (a + 1) * half)
                sq = jnp.maximum(sq_dist[pl.ds(at, 16), span], 1e-30)
                dist = sq * lax.rsqrt(sq)
                value = ((1.0 + dist + sq * (1.0 / 3.0)) * weight[a]) * jnp.exp(-dist)
                hi, lo = halves(value)
                k_hi[pl.ds(k * n + at, 16), span] = hi
                k_lo[pl.ds(k * n + at, 16), span] = lo
            return carry

        lax.fori_loop(0, n // 16, rows, 0)

    eye = lax.broadcasted_iota(jnp.int32, (m, 128), 0) == lax.broadcasted_iota(jnp.int32, (m, 128), 1)

    def to_row(column):
        return jnp.sum(jnp.where(eye, column, 0.0), axis=0, keepdims=True)

    def to_column(row):
        return jnp.sum(jnp.where(eye, row, 0.0), axis=1, keepdims=True)

    noise = noise_ref[...]
    residual = [vector_block(0, k) for k in range(nz)]
    direction = image = norm_now = None
    answer = jnp.zeros_like(own_probes)
    for t in range(ITERS):
        norm_part = sum(jnp.sum(r * r, axis=1, keepdims=True) for r in residual)
        rr_buf[t, 0] = to_row(norm_part)
        for j in range(1, nq):
            s = mirror_q(j)
            send(rr_buf.at[t, 0], rr_buf.at[t, s], rr_send.at[t, s], rr_recv.at[t, s], device(0, *q_offsets[j]))
        pieces = [halves(r) for r in residual]
        hi = jnp.concatenate([p[0] for p in pieces], axis=1)
        lo = jnp.concatenate([p[1] for p in pieces], axis=1)
        both = jnp.concatenate([hi, lo], axis=0)

        def partial(j):
            span = slice(j * n, (j + 1) * n)
            two = jnp.dot(both, k_hi[:, span], preferred_element_type=F32)
            return two[:m] + two[m:] + jnp.dot(hi, k_lo[:, span], preferred_element_type=F32)

        for j in reversed(range(1, nq)):
            part_out[t, j] = partial(j)
            s = mirror_q(j)
            send(part_out.at[t, j], part.at[t, s], part_send.at[t, s], part_recv.at[t, s], device(0, *q_offsets[j]))
        fresh = partial(0) + noise * residual[0]
        norm_row = rr_buf[t, 0]
        for j in range(1, nq):
            arrived(rr_buf.at[t, j], rr_send.at[t, j], rr_recv.at[t, j])
            norm_row = norm_row + rr_buf[t, j]
        norm_next = to_column(norm_row)
        for j in range(1, nq):
            arrived(part.at[t, j], part_send.at[t, j], part_recv.at[t, j])
            fresh = fresh + part[t, j]
        if t == 0:
            image, direction = fresh, residual
        else:
            beta = norm_next / norm_now
            image = fresh + beta * image
            direction = [r + beta * d for r, d in zip(residual, direction)]
        norm_now = norm_next
        if t + 1 < ITERS:
            vec[t + 1, 0] = image
            gather_vector(t + 1)
        dot_buf[t, 0] = to_row(jnp.sum(direction[0] * image, axis=1, keepdims=True))
        for i in range(1, nz * nq):
            s = mirror(i)
            send(dot_buf.at[t, 0], dot_buf.at[t, s], dot_send.at[t, s], dot_recv.at[t, s], device(*offsets[i]))
        dot_row = dot_buf[t, 0]
        for i in range(1, nz * nq):
            arrived(dot_buf.at[t, i], dot_send.at[t, i], dot_recv.at[t, i])
            dot_row = dot_row + dot_buf[t, i]
        alpha = norm_now / to_column(dot_row)
        answer = answer + alpha * direction[0]
        if t + 1 < ITERS:
            residual = [residual[0] - alpha * image] + [
                residual[k] - alpha * vector_block(t + 1, k) for k in range(1, nz)
            ]
        else:
            residual = [residual[0] - alpha * image]
    sol_ref[...] = answer.T
    res_ref[...] = residual[0].T
    for copy in sends:
        copy.wait_send()


def solution(mesh):
    ny = PAIR
    nz, ns = mesh.shape["pts"] // ny, mesh.shape["sub"]
    nq = ny * ns

    def local(points, inverse_scale, noise_level, probes, task_cov):
        n, features = points.shape
        m = probes.shape[1]
        depth = 3 * features + (-3 * features) % 128
        vmem = pl.BlockSpec(memory_space=pltpu.VMEM)
        dma = pltpu.SemaphoreType.DMA
        out = jax.ShapeDtypeStruct((n, m), F32)
        return pl.pallas_call(
            functools.partial(kernel, nz, ny, ns),
            out_shape=(out, out),
            in_specs=[vmem] * 4 + [pl.BlockSpec(memory_space=pltpu.SMEM)],
            out_specs=(vmem, vmem),
            scratch_shapes=[
                pltpu.VMEM((nz, features, n), F32),
                pltpu.VMEM((nq, features, n), F32),
                pltpu.VMEM((ITERS, nz, m, n), F32),
                pltpu.VMEM((ITERS, nq, m, n), F32),
                pltpu.VMEM((ITERS, nq, m, n), F32),
                pltpu.VMEM((ITERS, nq, 1, 128), F32),
                pltpu.VMEM((ITERS, nz * nq, 1, 128), F32),
                pltpu.VMEM((nz * n, nq * n), BF16),
                pltpu.VMEM((nz * n, nq * n), BF16),
                pltpu.VMEM((depth, nq * n), BF16),
                pltpu.VMEM((n, nq * n), F32),
                dma((nz,)), dma((nz,)), dma((nq,)), dma((nq,)),
                dma((ITERS, nz)), dma((ITERS, nz)),
                dma((ITERS, nq)), dma((ITERS, nq)),
                dma((ITERS, nq)), dma((ITERS, nq)),
                dma((ITERS, nz * nq)), dma((ITERS, nz * nq)),
            ],
            compiler_params=pltpu.CompilerParams(
                collective_id=0, has_side_effects=True, vmem_limit_bytes=48 * 2**20
            ),
        )(points, inverse_scale[None, :], noise_level[None, :], probes, task_cov)

    rows = P(("groups", "pts", "sub"), None)
    return jax.shard_map(
        local,
        mesh=mesh,
        in_specs=(rows, P(), P(("groups", "pts", "sub")), rows, P()),
        out_specs=(rows, rows),
        check_vma=False,
    )
```

```python
import functools

import jax
import jax.numpy as jnp
from jax import lax
from jax.experimental import pallas as pl
from jax.experimental.pallas import tpu as pltpu
from jax.sharding import PartitionSpec as P

ITERS = 3
PAIR = 2
MESH = pl.DeviceIdType.MESH
SQRT_FIVE = 5.0**0.5
F32, BF16 = jnp.float32, jnp.bfloat16


def halves(x):
    hi = x.astype(BF16)
    return hi, (x - hi.astype(F32)).astype(BF16)


def augmented(scaled):
    features, width = scaled.shape
    hi, lo = (part.astype(F32) for part in halves(scaled))
    square = jnp.sum(hi * hi + 2.0 * (hi * lo), axis=0, keepdims=True)
    top, rest = (part.astype(F32) for part in halves(square))
    mid = rest
    low = square - top - mid
    pad = (-3 * features) % 128
    row = lax.broadcasted_iota(jnp.int32, (pad, width), 0)
    three = jnp.where(row % 3 == 0, top, jnp.where(row % 3 == 1, mid, low))
    one = jnp.ones_like(three)
    zero = jnp.zeros_like(three)
    left = jnp.where(row < 3, three, jnp.where(row < 6, one, zero))
    right = jnp.where(row < 3, one, jnp.where(row < 6, three, zero))
    return (
        jnp.concatenate([-2.0 * hi, -2.0 * hi, -2.0 * lo, left], axis=0),
        jnp.concatenate([hi, lo, hi, right], axis=0),
    )


def kernel(
    nz, ny, ns, points_any, inverse_any, noise_any, probes_any, weights_any, sol_ref, res_ref,
    points_ref, inverse_ref, noise_ref, probes_ref, weights_ref, load_sem,
    col_pts, row_pts, vec, row_vec, part_out, part, dot_buf, k_hi, k_lo, right_fac, sq_dist,
    pts_z_send, pts_z_recv, pts_q_send, pts_q_recv, vec_send, vec_recv, row_send, row_recv,
    part_send, part_recv, dot_send, dot_recv,
):
    m, n = probes_ref.shape
    nq = ny * ns
    block = lax.axis_index("pts")
    core = lax.axis_index("sub")
    z, y = block // ny, block % ny

    def device(dz, a, b):
        return {"pts": ((z + dz) % nz) * ny + (y + a) % ny, "sub": (core + b) % ns}

    q_offsets = [(a, b) for a in range(ny) for b in range(ns)]
    offsets = [(dz, a, b) for dz in range(nz) for a, b in q_offsets]

    def mirror_q(j):
        a, b = q_offsets[j]
        return ((-a) % ny) * ns + (-b) % ns

    def mirror(i):
        dz, a, b = offsets[i]
        return ((-dz) % nz) * nq + mirror_q(a * ns + b)

    sends = []

    def send(src, dst, send_sem, recv_sem, target):
        copy = pltpu.make_async_remote_copy(
            src_ref=src, dst_ref=dst, send_sem=send_sem, recv_sem=recv_sem,
            device_id=target, device_id_type=MESH,
        )
        copy.start()
        sends.append(copy)

    def arrived(dst, send_sem, recv_sem):
        pltpu.make_async_remote_copy(
            src_ref=dst, dst_ref=dst, send_sem=send_sem, recv_sem=recv_sem,
            device_id=device(1, 0, 0), device_id_type=MESH,
        ).wait_recv()

    barrier = pltpu.get_barrier_semaphore()
    for i in range(1, nz * nq):
        pl.semaphore_signal(barrier, inc=1, device_id=device(*offsets[i]), device_id_type=MESH)

    loads = [
        pltpu.make_async_copy(src, dst, load_sem.at[i])
        for i, (src, dst) in enumerate((
            (points_any, points_ref), (inverse_any, inverse_ref), (probes_any, probes_ref),
            (noise_any, noise_ref), (weights_any, weights_ref),
        ))
    ]
    for load in loads:
        load.start()
    for load in loads:
        load.wait()
    scaled = points_ref[...] * (inverse_ref[...] * SQRT_FIVE).T
    col_pts[0] = scaled
    own_probes = probes_ref[...]
    vec[0, 0] = own_probes

    pl.semaphore_wait(barrier, nz * nq - 1)

    for dz in range(1, nz):
        k = nz - dz
        send(col_pts.at[0], col_pts.at[k], pts_z_send.at[k], pts_z_recv.at[k], device(dz, 0, 0))
    for j in range(1, nq):
        k = mirror_q(j)
        send(col_pts.at[0], row_pts.at[k], pts_q_send.at[k], pts_q_recv.at[k], device(0, *q_offsets[j]))

    def gather_vector(t):
        for dz in range(1, nz):
            k = nz - dz
            send(vec.at[t, 0], vec.at[t, k], vec_send.at[t, k], vec_recv.at[t, k], device(dz, 0, 0))
        for j in range(1, nq):
            k = mirror_q(j)
            send(vec.at[t, 0], row_vec.at[t, k], row_send.at[t, k], row_recv.at[t, k], device(0, *q_offsets[j]))

    def vector_block(t, k):
        if k:
            arrived(vec.at[t, k], vec_send.at[t, k], vec_recv.at[t, k])
        return vec[t, k]

    def row_block(t, j):
        if not j:
            return vec[t, 0]
        arrived(row_vec.at[t, j], row_send.at[t, j], row_recv.at[t, j])
        return row_vec[t, j]

    gather_vector(0)

    for j in range(nq):
        if j:
            arrived(row_pts.at[j], pts_q_send.at[j], pts_q_recv.at[j])
            factor = augmented(row_pts[j])[1]
        else:
            factor = augmented(scaled)[1]
        right_fac[:, j * n:(j + 1) * n] = factor.astype(BF16)

    half = ns * n
    for k in range(nz):
        if k:
            arrived(col_pts.at[k], pts_z_send.at[k], pts_z_recv.at[k])
        left = augmented(col_pts[k])[0].T.astype(BF16)
        sq_dist[...] = jnp.dot(left, right_fac[...], preferred_element_type=F32)
        column_block = ((z + k) % nz) * ny + y
        weight = [weights_ref[z * ny + (y + a) % ny, column_block] for a in range(ny)]

        def rows(i, carry):
            at = pl.multiple_of(i * 16, 16)
            for a in range(ny):
                span = slice(a * half, (a + 1) * half)
                sq = jnp.maximum(sq_dist[pl.ds(at, 16), span], 1e-30)
                dist = sq * lax.rsqrt(sq)
                value = ((1.0 + dist + sq * (1.0 / 3.0)) * weight[a]) * jnp.exp(-dist)
                hi, lo = halves(value)
                k_hi[pl.ds(k * n + at, 16), span] = hi
                k_lo[pl.ds(k * n + at, 16), span] = lo
            return carry

        lax.fori_loop(0, n // 16, rows, 0)

    line = lax.broadcasted_iota(jnp.int32, (m, 128), 0)
    lane = lax.broadcasted_iota(jnp.int32, (m, 128), 1)

    def to_row(columns):
        return sum(
            jnp.sum(jnp.where(lane == line + i * m, column, 0.0), axis=0, keepdims=True)
            for i, column in enumerate(columns)
        )

    def to_column(row, i):
        return jnp.sum(jnp.where(lane == line + i * m, row, 0.0), axis=1, keepdims=True)

    def total(x):
        return jnp.sum(x, axis=1, keepdims=True)

    noise = noise_ref[...]
    direction = image = norm_now = curve = None
    answer = jnp.zeros_like(own_probes)
    for t in range(ITERS):
        own = vec[t, 0]
        pieces = [halves(vector_block(t, k)) for k in range(nz)]
        hi = jnp.concatenate([p[0] for p in pieces], axis=1)
        lo = jnp.concatenate([p[1] for p in pieces], axis=1)
        both = jnp.concatenate([hi, lo], axis=0)

        def partial(j):
            span = slice(j * n, (j + 1) * n)
            two = jnp.dot(both, k_hi[:, span], preferred_element_type=F32)
            return two[:m] + two[m:] + jnp.dot(hi, k_lo[:, span], preferred_element_type=F32)

        products = jnp.zeros_like(own)
        for j in reversed(range(1, nq)):
            term = partial(j)
            part_out[t, j] = term
            s = mirror_q(j)
            send(part_out.at[t, j], part.at[t, s], part_send.at[t, s], part_recv.at[t, s], device(0, *q_offsets[j]))
            products = products + term * row_block(t, j)
        fresh = partial(0) + noise * own
        products = products + fresh * own
        crossed = own * image if t else jnp.zeros_like(own)
        dot_buf[t, 0] = to_row([total(products), total(own * own), total(crossed)])
        for i in reversed(range(1, nz * nq)):
            s = mirror(i)
            send(dot_buf.at[t, 0], dot_buf.at[t, s], dot_send.at[t, s], dot_recv.at[t, s], device(*offsets[i]))
        for j in range(1, nq):
            arrived(part.at[t, j], part_send.at[t, j], part_recv.at[t, j])
            fresh = fresh + part[t, j]
        sums = dot_buf[t, 0]
        for i in range(1, nz * nq):
            arrived(dot_buf.at[t, i], dot_send.at[t, i], dot_recv.at[t, i])
            sums = sums + dot_buf[t, i]
        norm_next = to_column(sums, 1)
        if t == 0:
            image, direction, curve = fresh, own, to_column(sums, 0)
        else:
            beta = norm_next / norm_now
            image = fresh + beta * image
            direction = own + beta * direction
            curve = to_column(sums, 0) + beta * (2.0 * to_column(sums, 2) + beta * curve)
        norm_now = norm_next
        alpha = norm_now / curve
        residual = own - alpha * image
        if t + 1 < ITERS:
            vec[t + 1, 0] = residual
            gather_vector(t + 1)
        answer = answer + alpha * direction
    sol_ref[...] = answer
    res_ref[...] = residual
    for copy in sends:
        copy.wait_send()


def solution(mesh):
    ny = PAIR
    nz, ns = mesh.shape["pts"] // ny, mesh.shape["sub"]
    nq = ny * ns

    def local(points, inverse_scale, noise_level, probes, task_cov):
        n, features = points.shape
        m = probes.shape[1]
        depth = 3 * features + (-3 * features) % 128
        vmem = pl.BlockSpec(memory_space=pltpu.VMEM)
        dma = pltpu.SemaphoreType.DMA
        out = jax.ShapeDtypeStruct((m, n), F32)
        answer, residual = pl.pallas_call(
            functools.partial(kernel, nz, ny, ns),
            out_shape=(out, out),
            in_specs=[pl.BlockSpec(memory_space=pltpu.HBM)] * 5,
            out_specs=(vmem, vmem),
            scratch_shapes=[
                pltpu.VMEM((features, n), F32),
                pltpu.VMEM((1, features), F32),
                pltpu.VMEM((1, n), F32),
                pltpu.VMEM((m, n), F32),
                pltpu.SMEM(task_cov.shape, F32),
                dma((5,)),
                pltpu.VMEM((nz, features, n), F32),
                pltpu.VMEM((nq, features, n), F32),
                pltpu.VMEM((ITERS, nz, m, n), F32),
                pltpu.VMEM((ITERS, nq, m, n), F32),
                pltpu.VMEM((ITERS, nq, m, n), F32),
                pltpu.VMEM((ITERS, nq, m, n), F32),
                pltpu.VMEM((ITERS, nz * nq, 1, 128), F32),
                pltpu.VMEM((nz * n, nq * n), BF16),
                pltpu.VMEM((nz * n, nq * n), BF16),
                pltpu.VMEM((depth, nq * n), BF16),
                pltpu.VMEM((n, nq * n), F32),
                dma((nz,)), dma((nz,)), dma((nq,)), dma((nq,)),
                dma((ITERS, nz)), dma((ITERS, nz)),
                dma((ITERS, nq)), dma((ITERS, nq)),
                dma((ITERS, nq)), dma((ITERS, nq)),
                dma((ITERS, nz * nq)), dma((ITERS, nz * nq)),
            ],
            compiler_params=pltpu.CompilerParams(
                collective_id=0, has_side_effects=True, vmem_limit_bytes=64 * 2**20
            ),
        )(points.T, inverse_scale[None, :], noise_level[None, :], probes.T, task_cov)
        return answer.T, residual.T

    rows = P(("groups", "pts", "sub"), None)
    return jax.shard_map(
        local,
        mesh=mesh,
        in_specs=(rows, P(), P(("groups", "pts", "sub")), rows, P()),
        out_specs=(rows, rows),
        check_vma=False,
    )
```

```python
import functools

import jax
import jax.numpy as jnp
from jax import lax
from jax.experimental import pallas as pl
from jax.experimental.pallas import tpu as pltpu
from jax.sharding import PartitionSpec as P

ITERS = 3
PAIR = 2
MESH = pl.DeviceIdType.MESH
SQRT_FIVE = 5.0**0.5
F32, BF16 = jnp.float32, jnp.bfloat16


def halves(x):
    hi = x.astype(BF16)
    return hi, (x - hi.astype(F32)).astype(BF16)


def augmented(scaled):
    features, width = scaled.shape
    hi, lo = (part.astype(F32) for part in halves(scaled))
    square = jnp.sum(hi * hi + 2.0 * (hi * lo), axis=0, keepdims=True)
    top, rest = (part.astype(F32) for part in halves(square))
    mid = rest
    low = square - top - mid
    pad = (-3 * features) % 128
    row = lax.broadcasted_iota(jnp.int32, (pad, width), 0)
    three = jnp.where(row % 3 == 0, top, jnp.where(row % 3 == 1, mid, low))
    one = jnp.ones_like(three)
    zero = jnp.zeros_like(three)
    left = jnp.where(row < 3, three, jnp.where(row < 6, one, zero))
    right = jnp.where(row < 3, one, jnp.where(row < 6, three, zero))
    return (
        jnp.concatenate([-2.0 * hi, -2.0 * hi, -2.0 * lo, left], axis=0),
        jnp.concatenate([hi, lo, hi, right], axis=0),
    )


def kernel(
    nz, ny, ns, points_any, inverse_any, noise_any, probes_any, weights_any, sol_ref, res_ref,
    points_ref, inverse_ref, noise_ref, probes_ref, weights_ref, load_sem,
    col_pts, row_pts, vec, row_vec, part_out, part, rr_buf, dot_buf, k_hi, k_lo, right_fac, sq_dist,
    pts_z_send, pts_z_recv, pts_q_send, pts_q_recv, vec_send, vec_recv, row_send, row_recv,
    part_send, part_recv, rr_send, rr_recv, dot_send, dot_recv,
):
    m, n = probes_ref.shape
    nq = ny * ns
    block = lax.axis_index("pts")
    core = lax.axis_index("sub")
    z, y = block // ny, block % ny

    def device(dz, a, b):
        return {"pts": ((z + dz) % nz) * ny + (y + a) % ny, "sub": (core + b) % ns}

    q_offsets = [(a, b) for a in range(ny) for b in range(ns)]
    offsets = [(dz, a, b) for dz in range(nz) for a, b in q_offsets]

    def mirror_q(j):
        a, b = q_offsets[j]
        return ((-a) % ny) * ns + (-b) % ns

    def mirror(i):
        dz, a, b = offsets[i]
        return ((-dz) % nz) * nq + mirror_q(a * ns + b)

    sends = []

    def send(src, dst, send_sem, recv_sem, target):
        copy = pltpu.make_async_remote_copy(
            src_ref=src, dst_ref=dst, send_sem=send_sem, recv_sem=recv_sem,
            device_id=target, device_id_type=MESH,
        )
        copy.start()
        sends.append(copy)

    def arrived(dst, send_sem, recv_sem):
        pltpu.make_async_remote_copy(
            src_ref=dst, dst_ref=dst, send_sem=send_sem, recv_sem=recv_sem,
            device_id=device(1, 0, 0), device_id_type=MESH,
        ).wait_recv()

    barrier = pltpu.get_barrier_semaphore()
    for i in range(1, nz * nq):
        pl.semaphore_signal(barrier, inc=1, device_id=device(*offsets[i]), device_id_type=MESH)

    loads = [
        pltpu.make_async_copy(src, dst, load_sem.at[i])
        for i, (src, dst) in enumerate((
            (points_any, points_ref), (inverse_any, inverse_ref), (probes_any, probes_ref),
            (noise_any, noise_ref), (weights_any, weights_ref),
        ))
    ]
    for load in loads:
        load.start()
    for load in loads:
        load.wait()
    scaled = points_ref[...] * (inverse_ref[...] * SQRT_FIVE).T
    col_pts[0] = scaled
    own_probes = probes_ref[...]
    vec[0, 0] = own_probes

    pl.semaphore_wait(barrier, nz * nq - 1)

    for dz in range(1, nz):
        k = nz - dz
        send(col_pts.at[0], col_pts.at[k], pts_z_send.at[k], pts_z_recv.at[k], device(dz, 0, 0))
    for j in range(1, nq):
        k = mirror_q(j)
        send(col_pts.at[0], row_pts.at[k], pts_q_send.at[k], pts_q_recv.at[k], device(0, *q_offsets[j]))

    def gather_vector(t):
        for dz in range(1, nz):
            k = nz - dz
            send(vec.at[t, 0], vec.at[t, k], vec_send.at[t, k], vec_recv.at[t, k], device(dz, 0, 0))
        for j in range(1, nq):
            k = mirror_q(j)
            send(vec.at[t, 0], row_vec.at[t, k], row_send.at[t, k], row_recv.at[t, k], device(0, *q_offsets[j]))

    def vector_block(t, k):
        if k:
            arrived(vec.at[t, k], vec_send.at[t, k], vec_recv.at[t, k])
        return vec[t, k]

    def row_block(t, j):
        if not j:
            return vec[t, 0]
        arrived(row_vec.at[t, j], row_send.at[t, j], row_recv.at[t, j])
        return row_vec[t, j]

    gather_vector(0)

    for j in range(nq):
        if j:
            arrived(row_pts.at[j], pts_q_send.at[j], pts_q_recv.at[j])
            factor = augmented(row_pts[j])[1]
        else:
            factor = augmented(scaled)[1]
        right_fac[:, j * n:(j + 1) * n] = factor.astype(BF16)

    half = ns * n
    for k in range(nz):
        if k:
            arrived(col_pts.at[k], pts_z_send.at[k], pts_z_recv.at[k])
        left = augmented(col_pts[k])[0].T.astype(BF16)
        sq_dist[...] = jnp.dot(left, right_fac[...], preferred_element_type=F32)
        column_block = ((z + k) % nz) * ny + y
        weight = [weights_ref[z * ny + (y + a) % ny, column_block] for a in range(ny)]

        def rows(i, carry):
            at = pl.multiple_of(i * 16, 16)
            for a in range(ny):
                span = slice(a * half, (a + 1) * half)
                sq = jnp.maximum(sq_dist[pl.ds(at, 16), span], 1e-30)
                dist = sq * lax.rsqrt(sq)
                value = ((1.0 + dist + sq * (1.0 / 3.0)) * weight[a]) * jnp.exp(-dist)
                hi, lo = halves(value)
                k_hi[pl.ds(k * n + at, 16), span] = hi
                k_lo[pl.ds(k * n + at, 16), span] = lo
            return carry

        lax.fori_loop(0, n // 16, rows, 0)

    line = lax.broadcasted_iota(jnp.int32, (m, 128), 0)
    lane = lax.broadcasted_iota(jnp.int32, (m, 128), 1)

    def to_row(columns):
        return sum(
            jnp.sum(jnp.where(lane == line + i * m, column, 0.0), axis=0, keepdims=True)
            for i, column in enumerate(columns)
        )

    def to_column(row, i):
        return jnp.sum(jnp.where(lane == line + i * m, row, 0.0), axis=1, keepdims=True)

    def total(x):
        return jnp.sum(x, axis=1, keepdims=True)

    noise = noise_ref[...]
    direction = image = norm_now = curve = None
    steps = []
    residual = [vector_block(0, k) for k in range(nz)]
    answer = jnp.zeros_like(own_probes)

    def send_dots(t):
        for i in reversed(range(1, nz * nq)):
            s = mirror(i)
            send(dot_buf.at[t, 0], dot_buf.at[t, s], dot_send.at[t, s], dot_recv.at[t, s], device(*offsets[i]))

    def sum_dots(t):
        sums = dot_buf[t, 0]
        for i in range(1, nz * nq):
            arrived(dot_buf.at[t, i], dot_send.at[t, i], dot_recv.at[t, i])
            sums = sums + dot_buf[t, i]
        return sums

    for t in range(ITERS):
        last = t + 1 == ITERS
        own = residual[0]
        if not last:
            rr_buf[t, 0] = to_row([sum(total(r * r) for r in residual)])
            for j in range(1, nq):
                s = mirror_q(j)
                send(rr_buf.at[t, 0], rr_buf.at[t, s], rr_send.at[t, s], rr_recv.at[t, s], device(0, *q_offsets[j]))
        pieces = [halves(r) for r in residual]
        hi = jnp.concatenate([p[0] for p in pieces], axis=1)
        lo = jnp.concatenate([p[1] for p in pieces], axis=1)
        both = jnp.concatenate([hi, lo], axis=0)

        def partial(j):
            span = slice(j * n, (j + 1) * n)
            two = jnp.dot(both, k_hi[:, span], preferred_element_type=F32)
            return two[:m] + two[m:] + jnp.dot(hi, k_lo[:, span], preferred_element_type=F32)

        products = jnp.zeros_like(own)
        for j in reversed(range(1, nq)):
            term = partial(j)
            part_out[t, j] = term
            s = mirror_q(j)
            send(part_out.at[t, j], part.at[t, s], part_send.at[t, s], part_recv.at[t, s], device(0, *q_offsets[j]))
            if last:
                row = row_block(0, j)
                for i, step in enumerate(steps):
                    row = row - step * row_block(i + 1, j)
                products = products + term * row
        fresh = partial(0) + noise * own
        if last:
            products = products + fresh * own
            crossed = own * image if t else jnp.zeros_like(own)
            dot_buf[t, 0] = to_row([total(products), total(own * own), total(crossed)])
            send_dots(t)
        else:
            norm_row = rr_buf[t, 0]
            for j in range(1, nq):
                arrived(rr_buf.at[t, j], rr_send.at[t, j], rr_recv.at[t, j])
                norm_row = norm_row + rr_buf[t, j]
            norm_next = to_column(norm_row, 0)
        for j in range(1, nq):
            arrived(part.at[t, j], part_send.at[t, j], part_recv.at[t, j])
            fresh = fresh + part[t, j]
        if last:
            sums = sum_dots(t)
            norm_next = to_column(sums, 1)
        if t == 0:
            image, direction = fresh, own
        else:
            beta = norm_next / norm_now
            image = fresh + beta * image
            direction = own + beta * direction
        if last:
            bent = to_column(sums, 0)
            curve = bent + beta * (2.0 * to_column(sums, 2) + beta * curve) if t else bent
        else:
            dot_buf[t, 0] = to_row([total(direction * image)])
            send_dots(t)
            vec[t + 1, 0] = image
            gather_vector(t + 1)
            curve = to_column(sum_dots(t), 0)
        norm_now = norm_next
        alpha = norm_now / curve
        steps.append(alpha)
        answer = answer + alpha * direction
        residual = [own - alpha * image] + [
            residual[k] - alpha * vector_block(t + 1, k) for k in range(1, 1 if last else nz)
        ]
    sol_ref[...] = answer
    res_ref[...] = residual[0]
    for copy in sends:
        copy.wait_send()


def solution(mesh):
    ny = PAIR
    nz, ns = mesh.shape["pts"] // ny, mesh.shape["sub"]
    nq = ny * ns

    def local(points, inverse_scale, noise_level, probes, task_cov):
        n, features = points.shape
        m = probes.shape[1]
        depth = 3 * features + (-3 * features) % 128
        vmem = pl.BlockSpec(memory_space=pltpu.VMEM)
        dma = pltpu.SemaphoreType.DMA
        out = jax.ShapeDtypeStruct((m, n), F32)
        answer, residual = pl.pallas_call(
            functools.partial(kernel, nz, ny, ns),
            out_shape=(out, out),
            in_specs=[pl.BlockSpec(memory_space=pltpu.HBM)] * 5,
            out_specs=(vmem, vmem),
            scratch_shapes=[
                pltpu.VMEM((features, n), F32),
                pltpu.VMEM((1, features), F32),
                pltpu.VMEM((1, n), F32),
                pltpu.VMEM((m, n), F32),
                pltpu.SMEM(task_cov.shape, F32),
                dma((5,)),
                pltpu.VMEM((nz, features, n), F32),
                pltpu.VMEM((nq, features, n), F32),
                pltpu.VMEM((ITERS, nz, m, n), F32),
                pltpu.VMEM((ITERS, nq, m, n), F32),
                pltpu.VMEM((ITERS, nq, m, n), F32),
                pltpu.VMEM((ITERS, nq, m, n), F32),
                pltpu.VMEM((ITERS, nq, 1, 128), F32),
                pltpu.VMEM((ITERS, nz * nq, 1, 128), F32),
                pltpu.VMEM((nz * n, nq * n), BF16),
                pltpu.VMEM((nz * n, nq * n), BF16),
                pltpu.VMEM((depth, nq * n), BF16),
                pltpu.VMEM((n, nq * n), F32),
                dma((nz,)), dma((nz,)), dma((nq,)), dma((nq,)),
                dma((ITERS, nz)), dma((ITERS, nz)),
                dma((ITERS, nq)), dma((ITERS, nq)),
                dma((ITERS, nq)), dma((ITERS, nq)),
                dma((ITERS, nq)), dma((ITERS, nq)),
                dma((ITERS, nz * nq)), dma((ITERS, nz * nq)),
            ],
            compiler_params=pltpu.CompilerParams(
                collective_id=0, has_side_effects=True, vmem_limit_bytes=64 * 2**20
            ),
        )(points.T, inverse_scale[None, :], noise_level[None, :], probes.T, task_cov)
        return answer.T, residual.T

    rows = P(("groups", "pts", "sub"), None)
    return jax.shard_map(
        local,
        mesh=mesh,
        in_specs=(rows, P(), P(("groups", "pts", "sub")), rows, P()),
        out_specs=(rows, rows),
        check_vma=False,
    )
```

```python
import functools

import jax
import jax.numpy as jnp
from jax import lax
from jax.experimental import pallas as pl
from jax.experimental.pallas import tpu as pltpu
from jax.sharding import PartitionSpec as P

ITERS = 3
PAIR = 2
MESH = pl.DeviceIdType.MESH
SQRT_FIVE = 5.0**0.5
F32, BF16 = jnp.float32, jnp.bfloat16


def halves(x):
    hi = x.astype(BF16)
    return hi, (x - hi.astype(F32)).astype(BF16)


def augmented(scaled):
    features, width = scaled.shape
    hi, lo = (part.astype(F32) for part in halves(scaled))
    square = jnp.sum(hi * hi + 2.0 * (hi * lo), axis=0, keepdims=True)
    top, rest = (part.astype(F32) for part in halves(square))
    mid = rest
    low = square - top - mid
    pad = (-3 * features) % 128
    row = lax.broadcasted_iota(jnp.int32, (pad, width), 0)
    three = jnp.where(row % 3 == 0, top, jnp.where(row % 3 == 1, mid, low))
    one = jnp.ones_like(three)
    zero = jnp.zeros_like(three)
    left = jnp.where(row < 3, three, jnp.where(row < 6, one, zero))
    right = jnp.where(row < 3, one, jnp.where(row < 6, three, zero))
    return (
        jnp.concatenate([-2.0 * hi, -2.0 * hi, -2.0 * lo, left], axis=0),
        jnp.concatenate([hi, lo, hi, right], axis=0),
    )


def kernel(
    nz, ny, ns, points_any, inverse_any, noise_any, probes_any, weights_any, sol_ref, res_ref,
    points_ref, inverse_ref, noise_ref, probes_ref, weights_ref, load_sem,
    col_pts, row_pts, vec, row_vec, part_out, part, rr_buf, dot_buf, k_hi, k_lo, right_fac, sq_dist,
    pts_z_send, pts_z_recv, pts_q_send, pts_q_recv, vec_send, vec_recv, row_send, row_recv,
    part_send, part_recv, rr_send, rr_recv, dot_send, dot_recv,
):
    m, n = probes_ref.shape
    nq = ny * ns
    block = lax.axis_index("pts")
    core = lax.axis_index("sub")
    z, y = block // ny, block % ny

    def device(dz, a, b):
        return {"pts": ((z + dz) % nz) * ny + (y + a) % ny, "sub": (core + b) % ns}

    q_offsets = [(a, b) for a in range(ny) for b in range(ns)]
    offsets = [(dz, a, b) for dz in range(nz) for a, b in q_offsets]

    def mirror_q(j):
        a, b = q_offsets[j]
        return ((-a) % ny) * ns + (-b) % ns

    def mirror(i):
        dz, a, b = offsets[i]
        return ((-dz) % nz) * nq + mirror_q(a * ns + b)

    sends = []

    def send(src, dst, send_sem, recv_sem, target):
        copy = pltpu.make_async_remote_copy(
            src_ref=src, dst_ref=dst, send_sem=send_sem, recv_sem=recv_sem,
            device_id=target, device_id_type=MESH,
        )
        copy.start()
        sends.append(copy)

    def arrived(dst, send_sem, recv_sem):
        pltpu.make_async_remote_copy(
            src_ref=dst, dst_ref=dst, send_sem=send_sem, recv_sem=recv_sem,
            device_id=device(1, 0, 0), device_id_type=MESH,
        ).wait_recv()

    barrier = pltpu.get_barrier_semaphore()
    for i in range(1, nz * nq):
        pl.semaphore_signal(barrier, inc=1, device_id=device(*offsets[i]), device_id_type=MESH)

    loads = [
        pltpu.make_async_copy(src, dst, load_sem.at[i])
        for i, (src, dst) in enumerate((
            (points_any, points_ref), (inverse_any, inverse_ref), (probes_any, probes_ref),
            (noise_any, noise_ref), (weights_any, weights_ref),
        ))
    ]
    for load in loads:
        load.start()
    for load in loads:
        load.wait()
    scaled = points_ref[...] * (inverse_ref[...] * SQRT_FIVE).T
    col_pts[0] = scaled
    own_probes = probes_ref[...]
    vec[0, 0] = own_probes

    pl.semaphore_wait(barrier, nz * nq - 1)

    for dz in range(1, nz):
        k = nz - dz
        send(col_pts.at[0], col_pts.at[k], pts_z_send.at[k], pts_z_recv.at[k], device(dz, 0, 0))
    for j in range(1, nq):
        k = mirror_q(j)
        send(col_pts.at[0], row_pts.at[k], pts_q_send.at[k], pts_q_recv.at[k], device(0, *q_offsets[j]))

    def gather_vector(t):
        for dz in range(1, nz):
            k = nz - dz
            send(vec.at[t, 0], vec.at[t, k], vec_send.at[t, k], vec_recv.at[t, k], device(dz, 0, 0))
        for j in range(1, nq):
            k = mirror_q(j)
            send(vec.at[t, 0], row_vec.at[t, k], row_send.at[t, k], row_recv.at[t, k], device(0, *q_offsets[j]))

    def vector_block(t, k):
        if k:
            arrived(vec.at[t, k], vec_send.at[t, k], vec_recv.at[t, k])
        return vec[t, k]

    def row_block(t, j):
        if not j:
            return vec[t, 0]
        arrived(row_vec.at[t, j], row_send.at[t, j], row_recv.at[t, j])
        return row_vec[t, j]

    gather_vector(0)

    for j in range(nq):
        if j:
            arrived(row_pts.at[j], pts_q_send.at[j], pts_q_recv.at[j])
            factor = augmented(row_pts[j])[1]
        else:
            factor = augmented(scaled)[1]
        right_fac[:, j * n:(j + 1) * n] = factor.astype(BF16)

    half = ns * n
    for k in range(nz):
        if k:
            arrived(col_pts.at[k], pts_z_send.at[k], pts_z_recv.at[k])
        left = augmented(col_pts[k])[0].T.astype(BF16)
        sq_dist[...] = jnp.dot(left, right_fac[...], preferred_element_type=F32)
        column_block = ((z + k) % nz) * ny + y
        weight = [weights_ref[z * ny + (y + a) % ny, column_block] for a in range(ny)]

        def rows(i, carry):
            at = pl.multiple_of(i * 16, 16)
            for a in range(ny):
                span = slice(a * half, (a + 1) * half)
                sq = jnp.maximum(sq_dist[pl.ds(at, 16), span], 1e-30)
                dist = sq * lax.rsqrt(sq)
                value = ((1.0 + dist + sq * (1.0 / 3.0)) * weight[a]) * jnp.exp(-dist)
                hi, lo = halves(value)
                k_hi[pl.ds(k * n + at, 16), span] = hi
                k_lo[pl.ds(k * n + at, 16), span] = lo
            return carry

        lax.fori_loop(0, n // 16, rows, 0, unroll=4)

    line = lax.broadcasted_iota(jnp.int32, (m, 128), 0)
    lane = lax.broadcasted_iota(jnp.int32, (m, 128), 1)

    def to_row(columns):
        return sum(
            jnp.sum(jnp.where(lane == line + i * m, column, 0.0), axis=0, keepdims=True)
            for i, column in enumerate(columns)
        )

    def to_column(row, i):
        return jnp.sum(jnp.where(lane == line + i * m, row, 0.0), axis=1, keepdims=True)

    def total(x):
        return jnp.sum(x, axis=1, keepdims=True)

    noise = noise_ref[...]
    direction = image = norm_now = curve = None
    steps = []
    residual = [vector_block(0, k) for k in range(nz)]
    answer = jnp.zeros_like(own_probes)

    def send_dots(t):
        for i in reversed(range(1, nz * nq)):
            s = mirror(i)
            send(dot_buf.at[t, 0], dot_buf.at[t, s], dot_send.at[t, s], dot_recv.at[t, s], device(*offsets[i]))

    def sum_dots(t):
        sums = dot_buf[t, 0]
        for i in range(1, nz * nq):
            arrived(dot_buf.at[t, i], dot_send.at[t, i], dot_recv.at[t, i])
            sums = sums + dot_buf[t, i]
        return sums

    for t in range(ITERS):
        last = t + 1 == ITERS
        own = residual[0]
        if not last:
            rr_buf[t, 0] = to_row([sum(total(r * r) for r in residual)])
            for j in range(1, nq):
                s = mirror_q(j)
                send(rr_buf.at[t, 0], rr_buf.at[t, s], rr_send.at[t, s], rr_recv.at[t, s], device(0, *q_offsets[j]))
        pieces = [halves(r) for r in residual]
        hi = jnp.concatenate([p[0] for p in pieces], axis=1)
        lo = jnp.concatenate([p[1] for p in pieces], axis=1)
        both = jnp.concatenate([hi, lo], axis=0)

        def partial(j):
            span = slice(j * n, (j + 1) * n)
            two = jnp.dot(both, k_hi[:, span], preferred_element_type=F32)
            return two[:m] + two[m:] + jnp.dot(hi, k_lo[:, span], preferred_element_type=F32)

        products = jnp.zeros_like(own)
        for j in reversed(range(1, nq)):
            term = partial(j)
            part_out[t, j] = term
            s = mirror_q(j)
            send(part_out.at[t, j], part.at[t, s], part_send.at[t, s], part_recv.at[t, s], device(0, *q_offsets[j]))
            if last:
                row = row_block(0, j)
                for i, step in enumerate(steps):
                    row = row - step * row_block(i + 1, j)
                products = products + term * row
        fresh = partial(0) + noise * own
        if last:
            products = products + fresh * own
            crossed = own * image if t else jnp.zeros_like(own)
            dot_buf[t, 0] = to_row([total(products), total(own * own), total(crossed)])
            send_dots(t)
        else:
            norm_row = rr_buf[t, 0]
            for j in range(1, nq):
                arrived(rr_buf.at[t, j], rr_send.at[t, j], rr_recv.at[t, j])
                norm_row = norm_row + rr_buf[t, j]
            norm_next = to_column(norm_row, 0)
        for j in range(1, nq):
            arrived(part.at[t, j], part_send.at[t, j], part_recv.at[t, j])
            fresh = fresh + part[t, j]
        if last:
            sums = sum_dots(t)
            norm_next = to_column(sums, 1)
        if t == 0:
            image, direction = fresh, own
        else:
            beta = norm_next / norm_now
            image = fresh + beta * image
            direction = own + beta * direction
        if last:
            bent = to_column(sums, 0)
            curve = bent + beta * (2.0 * to_column(sums, 2) + beta * curve) if t else bent
        else:
            dot_buf[t, 0] = to_row([total(direction * image)])
            send_dots(t)
            vec[t + 1, 0] = image
            gather_vector(t + 1)
            curve = to_column(sum_dots(t), 0)
        norm_now = norm_next
        alpha = norm_now / curve
        steps.append(alpha)
        answer = answer + alpha * direction
        residual = [own - alpha * image] + [
            residual[k] - alpha * vector_block(t + 1, k) for k in range(1, 1 if last else nz)
        ]
    sol_ref[...] = answer
    res_ref[...] = residual[0]
    for copy in sends:
        copy.wait_send()


def solution(mesh):
    ny = PAIR
    nz, ns = mesh.shape["pts"] // ny, mesh.shape["sub"]
    nq = ny * ns

    def local(points, inverse_scale, noise_level, probes, task_cov):
        n, features = points.shape
        m = probes.shape[1]
        depth = 3 * features + (-3 * features) % 128
        vmem = pl.BlockSpec(memory_space=pltpu.VMEM)
        dma = pltpu.SemaphoreType.DMA
        out = jax.ShapeDtypeStruct((m, n), F32)
        answer, residual = pl.pallas_call(
            functools.partial(kernel, nz, ny, ns),
            out_shape=(out, out),
            in_specs=[pl.BlockSpec(memory_space=pltpu.HBM)] * 5,
            out_specs=(vmem, vmem),
            scratch_shapes=[
                pltpu.VMEM((features, n), F32),
                pltpu.VMEM((1, features), F32),
                pltpu.VMEM((1, n), F32),
                pltpu.VMEM((m, n), F32),
                pltpu.SMEM(task_cov.shape, F32),
                dma((5,)),
                pltpu.VMEM((nz, features, n), F32),
                pltpu.VMEM((nq, features, n), F32),
                pltpu.VMEM((ITERS, nz, m, n), F32),
                pltpu.VMEM((ITERS, nq, m, n), F32),
                pltpu.VMEM((ITERS, nq, m, n), F32),
                pltpu.VMEM((ITERS, nq, m, n), F32),
                pltpu.VMEM((ITERS, nq, 1, 128), F32),
                pltpu.VMEM((ITERS, nz * nq, 1, 128), F32),
                pltpu.VMEM((nz * n, nq * n), BF16),
                pltpu.VMEM((nz * n, nq * n), BF16),
                pltpu.VMEM((depth, nq * n), BF16),
                pltpu.VMEM((n, nq * n), F32),
                dma((nz,)), dma((nz,)), dma((nq,)), dma((nq,)),
                dma((ITERS, nz)), dma((ITERS, nz)),
                dma((ITERS, nq)), dma((ITERS, nq)),
                dma((ITERS, nq)), dma((ITERS, nq)),
                dma((ITERS, nq)), dma((ITERS, nq)),
                dma((ITERS, nz * nq)), dma((ITERS, nz * nq)),
            ],
            compiler_params=pltpu.CompilerParams(
                collective_id=0, has_side_effects=True, vmem_limit_bytes=64 * 2**20
            ),
        )(points.T, inverse_scale[None, :], noise_level[None, :], probes.T, task_cov)
        return answer.T, residual.T

    rows = P(("groups", "pts", "sub"), None)
    return jax.shard_map(
        local,
        mesh=mesh,
        in_specs=(rows, P(), P(("groups", "pts", "sub")), rows, P()),
        out_specs=(rows, rows),
        check_vma=False,
    )
```
